512 devices in a mesh: seq: 64 (over y, x, core), tp: 8 (over z).
Axes of the slice: x: 4, y: 8, z: 8, core: 2. Of those that a mesh axis runs over, the one named last changes fastest.
Arguments:
- queries: bfloat16 [32768, 4096], P('seq', 'tp'), may hold values from -9 to 9
- keys: bfloat16 [32768, 4096], P('seq', 'tp'), may hold values from -9 to 9
- values: bfloat16 [32768, 4096], P('seq', 'tp'), may hold values from -6 to 6
- route: int32 [32, 32768], P('tp', 'seq'), may hold values from 0 to 32767, as said below
- members: int32 [32, 32768], P('tp', 'seq'), may hold values from 0 to 32767, as said below
- pattern: int32 [32, 128, 10], P('tp', 'seq'), may hold values from 0 to 1, as said below
- w_out: bfloat16 [4096, 4096], P('tp', 'seq'), may hold values from -0.25 to 0.25
Outputs:
- mixed: bfloat16 [32768, 4096], P('seq', 'tp')
The draws below stay inside these ranges and needn't reach their ends.
Inputs may be any that keep to these rules, and one draw needn't show every extreme that they name: `route`: each row is a permutation of the positions; for every aligned block of 512 positions and every aligned block of 512 slots, exactly 8 of the block's positions have their slot in that slot block. members[h] is the inverse permutation of route[h]: members[h, route[h, p]] = p. `pattern`: entries 2 * 2 and 2 * 2 + 1 (the cluster's own blocks) are always 1; entries whose cluster lies outside 0 to 127 are always 0.
All inputs are finite; a program needn't handle non-finite values.
Results may differ from the reference program's by a relative error of at most 0.017.
Values may be sent and summed in bfloat16 or wider, within the bound.
A program may use at most 64 MiB of HBM per device.

```python
import jax
import jax.numpy as jnp
from jax import lax

D = 4096
H = 32
HEAD = 128
CLUSTER = 256
BLOCK = 128
REACH = 2
TOK_DEV = 512
TOKENS = 32768
NCLUST = 128
N_TP = 8


def routing_tables(key):
    base_key = jax.random.fold_in(key, 7001)
    device_count = TOKENS // TOK_DEV
    per_peer = TOK_DEV // device_count

    def one_head(head_key):
        send_keys = jax.random.split(jax.random.fold_in(head_key, 1), device_count)
        land_keys = jax.random.split(jax.random.fold_in(head_key, 2), device_count)
        shuffle_send = jax.vmap(lambda inner_key: jax.random.permutation(inner_key, TOK_DEV))(send_keys).astype(jnp.int32)
        shuffle_land = jax.vmap(lambda inner_key: jax.random.permutation(inner_key, TOK_DEV))(land_keys).astype(jnp.int32)
        source = jnp.arange(device_count, dtype=jnp.int32)[:, None]
        sent_index = jnp.arange(TOK_DEV, dtype=jnp.int32)[None, :]
        target = sent_index // per_peer
        arrival = source * per_peer + sent_index % per_peer
        slots = target * TOK_DEV + shuffle_land[target, arrival]
        positions = source * TOK_DEV + shuffle_send
        route_row = jnp.zeros((TOKENS,), jnp.int32).at[positions.reshape(-1)].set(slots.reshape(-1).astype(jnp.int32))
        member_row = jnp.zeros((TOKENS,), jnp.int32).at[slots.reshape(-1)].set(positions.reshape(-1).astype(jnp.int32))
        return (route_row, member_row)
    return jax.vmap(one_head)(jax.random.split(base_key, H))


def draw_route(key, part):
    return routing_tables(key)[0]


def draw_members(key, part):
    return routing_tables(key)[1]


def draw_pattern(key, part):
    block_count = 4 * REACH + 2
    random_bits = jax.random.randint(jax.random.fold_in(key, 7002), (H, NCLUST, block_count), 0, 2).astype(jnp.int32)
    block_index = jnp.arange(block_count, dtype=jnp.int32)[None, None, :]
    cluster_index = jnp.arange(NCLUST, dtype=jnp.int32)[None, :, None]
    neighbour = cluster_index + block_index // 2 - REACH
    inside = (neighbour >= 0) & (neighbour < NCLUST)
    own_block = block_index // 2 == REACH
    return jnp.where(own_block, 1, jnp.where(inside, random_bits, 0)).astype(jnp.int32)


def attention_inputs(key):
    shape = (TOKENS, H, HEAD)
    query_key = jax.random.fold_in(key, 7003)
    other_key = jax.random.fold_in(key, 7004)
    query_base = jax.random.truncated_normal(query_key, -6.0, 6.0, shape, jnp.float32)
    key_base = jax.random.truncated_normal(other_key, -6.0, 6.0, shape, jnp.float32)
    return (query_base.reshape(TOKENS, H * HEAD), key_base.reshape(TOKENS, H * HEAD))


def draw_queries(key, part):
    return attention_inputs(key)[0].astype(jnp.bfloat16)


def draw_keys(key, part):
    return attention_inputs(key)[1].astype(jnp.bfloat16)


def strengthened(values, own_key, source, target, shards_of, factor):
    owner, partner = [(jnp.arange(values.shape[axis_at]) // (values.shape[axis_at] // shards_of)).reshape([-1 if axis == axis_at else 1 for axis in range(values.ndim)]) for axis_at in (source, target)]
    chosen = jax.random.permutation(own_key, shards_of)[partner]
    strong = (owner == chosen) | (owner == (partner + shards_of // 2) % shards_of)
    return jnp.where(strong, factor * values, values)


def level_of(own_key, shape, shards, least, high):
    level = 1.0
    for position, blocks in shards:
        draws = jax.random.uniform(jax.random.fold_in(jax.random.fold_in(own_key, 6), position), (blocks,), jnp.float32, least / len(shards), high / len(shards))
        level = level * jnp.repeat(jnp.exp(draws), shape[position] // blocks).reshape((-1,) + (1,) * (len(shape) - 1 - position))
    return level


def centred(key, dims, deviation, bound, cuts=(), kind=jnp.bfloat16):
    gain = level_of(key, dims, cuts, -0.22, 0.18) if cuts else 1.0
    entries = jax.random.normal(key, dims, jnp.float32) * deviation * gain
    return jnp.minimum(jnp.maximum(entries, -bound), bound).astype(kind)


def noise_with(key, dims, scale, most, cuts, heavy, kind=jnp.bfloat16):
    result = scale * jax.random.normal(key, dims, jnp.float32)
    if cuts:
        result = result * level_of(key, dims, cuts, -0.22, 0.18)
    return jnp.clip(strengthened(result, jax.random.fold_in(key, 3), *heavy), -most, most).astype(kind)


def setup_inputs(seed: int = 0) -> dict:
    splits = jax.random.split(jax.random.key(seed), 8)
    queries = draw_queries(jax.random.fold_in(splits[7], 71), 0)
    keys = draw_keys(jax.random.fold_in(splits[7], 71), 0)
    values = centred(splits[2], (TOKENS, H * HEAD), 1.0, 6.0, ((0, 64), (1, 8)))
    route = draw_route(jax.random.fold_in(splits[7], 71), 0)
    members = draw_members(jax.random.fold_in(splits[7], 71), 0)
    pattern = draw_pattern(jax.random.fold_in(splits[7], 71), 0)
    w_out = noise_with(splits[6], (H * HEAD, D), (H * HEAD) ** -0.5, 0.25, ((0, 8), (1, 64)), (0, 1, 64, 4.0))
    return {"queries": queries, "keys": keys, "values": values, "route": route, "members": members, "pattern": pattern, "w_out": w_out}


def window_attention(pieces):
    query_head, key_head, value_head, member_row, route_row, pattern_head = pieces
    ordered_query = jnp.take(query_head, member_row, axis=0)
    ordered_key = jnp.take(key_head, member_row, axis=0)
    ordered_value = jnp.take(value_head, member_row, axis=0)
    cluster_count = ordered_query.shape[0] // CLUSTER
    window_rows = (2 * REACH + 1) * CLUSTER
    zero_rim = jnp.zeros((REACH * CLUSTER, HEAD), ordered_key.dtype)
    padded_key = jnp.concatenate([zero_rim, ordered_key, zero_rim], axis=0)
    padded_value = jnp.concatenate([zero_rim, ordered_value, zero_rim], axis=0)
    starts = (jnp.arange(cluster_count) * CLUSTER).astype(jnp.int32)
    key_window = jax.vmap(lambda slot_start: lax.dynamic_slice_in_dim(padded_key, slot_start, window_rows, 0))(starts)
    value_window = jax.vmap(lambda slot_start: lax.dynamic_slice_in_dim(padded_value, slot_start, window_rows, 0))(starts)
    query_blocks = ordered_query.reshape(cluster_count, CLUSTER, HEAD)
    scores = jnp.einsum("cqd,ckd->cqk", query_blocks.astype(jnp.float32), key_window.astype(jnp.float32)) * (HEAD ** -0.5)
    allowed = jnp.repeat(pattern_head, BLOCK, axis=1) > 0
    scores = jnp.where(allowed[:, None, :], scores, -jnp.inf)
    row_max = jnp.max(scores, axis=-1, keepdims=True)
    exponent = jnp.exp(scores - row_max)
    weights = (exponent / jnp.sum(exponent, axis=-1, keepdims=True)).astype(jnp.bfloat16)
    context = jnp.einsum("cqk,ckd->cqd", weights.astype(jnp.float32), value_window.astype(jnp.float32)).astype(jnp.bfloat16)
    context = context.reshape(cluster_count * CLUSTER, HEAD)
    return jnp.take(context, route_row, axis=0)


def reference(queries, keys, values, route, members, pattern, w_out):
    token_count = queries.shape[0]

    def by_head(input_array):
        return input_array.reshape(token_count, H, HEAD).transpose(1, 0, 2)

    context = lax.map(window_attention, (by_head(queries), by_head(keys), by_head(values), members, route, pattern))
    attended = context.transpose(1, 0, 2).reshape(token_count, H * HEAD)
    group_width = (H // N_TP) * HEAD
    summed = jnp.zeros((token_count, D), jnp.float32)
    for group_index in range(N_TP):
        lower_edge = group_index * group_width
        partial_value = jnp.dot(attended[:, lower_edge:lower_edge + group_width], w_out[lower_edge:lower_edge + group_width], preferred_element_type=jnp.float32)
        rounded = lax.optimization_barrier(partial_value.astype(jnp.bfloat16))
        summed = summed + rounded.astype(jnp.float32)
    return summed.astype(jnp.bfloat16)
```

```python
import functools

import jax
import jax.numpy as jnp
from jax import lax
from jax.experimental import pallas as pl
from jax.experimental.pallas import tpu as pltpu
from jax.sharding import PartitionSpec as P

MESH = pl.DeviceIdType.MESH
HEAD = 128
CLUSTER = 256
BLOCK = 128
WINDOW = 5 * CLUSTER
LOG2E = 1.4426950408889634


def dot(a, b, contract=((1,), (0,))):
    return lax.dot_general(a, b, (contract, ((), ())), preferred_element_type=jnp.float32)


def attention_kernel(
    peers, planes, heads,
    q_ref, k_ref, v_ref, route_ref, members_ref, pattern_ref,
    gathered,
    index_row, index_col, packed, arrived, query, window, context, leaving, returned,
    send_q, recv_q, send_h, recv_h, send_c, recv_c, send_z, recv_z,
):
    rows = q_ref.shape[0]
    share = rows // peers
    me = lax.axis_index("seq")
    plane = lax.axis_index("tp")
    after, before = lax.rem(me + 1, peers), lax.rem(me + peers - 1, peers)
    above, below = lax.rem(plane + 1, planes), lax.rem(plane + planes - 1, planes)

    barrier = pltpu.get_barrier_semaphore()

    def greet(i, carry):
        pl.semaphore_signal(
            barrier, inc=1, device_id={"seq": lax.rem(me + i, peers)}, device_id_type=MESH
        )
        return carry

    lax.fori_loop(1, peers, greet, 0)
    for other in (above, below):
        pl.semaphore_signal(barrier, inc=1, device_id={"tp": other}, device_id_type=MESH)

    slot = lax.broadcasted_iota(jnp.int32, members_ref.shape, 1)
    order = jnp.concatenate(
        [route_ref[...], lax.div(members_ref[...], rows) * rows + slot], axis=0
    ).astype(jnp.float32)
    order_col = order.T
    ranks = []
    for i in range(2 * heads):
        smaller = order_col[:, i : i + 1] < order[i : i + 1, :]
        ranks.append(jnp.sum(smaller.astype(jnp.float32), axis=0, keepdims=True))
    ranks = jnp.concatenate(ranks, axis=0)
    index_row[...] = ranks.astype(jnp.int32)
    index_col[...] = ranks.T.astype(jnp.int32)

    def table(i):
        at = lax.broadcasted_iota(jnp.int32, (rows, rows), 0)
        return (at == index_row[i : i + 1, :]).astype(jnp.bfloat16)

    def table_t(i):
        at = lax.broadcasted_iota(jnp.int32, (rows, rows), 1)
        return (at == index_col[:, i : i + 1]).astype(jnp.bfloat16)

    def to_all(source, landing, send_sem, recv_sem, h):
        def send(i, carry):
            peer = lax.rem(me + i, peers)
            pltpu.make_async_remote_copy(
                src_ref=source.at[h, peer], dst_ref=landing.at[h, me],
                send_sem=send_sem.at[h], recv_sem=recv_sem.at[h],
                device_id={"seq": peer}, device_id_type=MESH,
            ).start()
            return carry

        lax.fori_loop(1, peers, send, 0)
        landing[h, me] = source[h, me]

    def all_of(source, landing, send_sem, recv_sem, h):
        others = pl.ds(0, peers - 1)
        return pltpu.make_async_remote_copy(
            src_ref=source.at[h, others], dst_ref=landing.at[h, others],
            send_sem=send_sem.at[h], recv_sem=recv_sem.at[h],
            device_id={"seq": after}, device_id_type=MESH,
        )

    def halo(h, side):
        own = window.at[h, pl.ds(rows, rows)]
        landing = window.at[h, pl.ds(0 if side == 0 else 2 * rows, rows)]
        return pltpu.make_async_remote_copy(
            src_ref=own, dst_ref=landing,
            send_sem=send_h.at[h, side], recv_sem=recv_h.at[h, side],
            device_id={"seq": after if side == 0 else before}, device_id_type=MESH,
        )

    def hops(h, way):
        return planes // 2 - (h + way) % 2

    def ring(h, way, hop):
        held = lax.rem(plane + planes - hop if way == 0 else plane + hop, planes)
        block = gathered.at[held, h]
        return pltpu.make_async_remote_copy(
            src_ref=block, dst_ref=block,
            send_sem=send_z.at[h, way, hop], recv_sem=recv_z.at[h, way, hop],
            device_id={"tp": above if way == 0 else below}, device_id_type=MESH,
        )

    def send_qkv(h):
        columns = slice(h * HEAD, (h + 1) * HEAD)
        stacked = jnp.concatenate([q_ref[:, columns], k_ref[:, columns], v_ref[:, columns]], axis=1)
        packed[h] = dot(table(h), stacked).reshape(peers, share, 3 * HEAD).astype(jnp.bfloat16)

    def start_qkv(h):
        to_all(packed, arrived, send_q, recv_q, h)

    def land(h):
        all_of(packed, arrived, send_q, recv_q, h).wait_recv()
        came = arrived[h].astype(jnp.float32).reshape(rows, 3 * HEAD).astype(jnp.bfloat16)
        placed = dot(table_t(heads + h), came).astype(jnp.bfloat16)
        query[h] = placed[:, :HEAD]
        window[h, pl.ds(rows, rows)] = placed[:, HEAD:]
        halo(h, 0).start()
        halo(h, 1).start()

    def attend(h):
        halo(h, 0).wait_recv()
        halo(h, 1).wait_recv()

        def cluster(c, carry):
            start = pl.multiple_of(c * CLUSTER, CLUSTER)
            q = query[h, pl.ds(start, CLUSTER)]
            kv = window.at[h, pl.ds(start, WINDOW)]
            scores = dot(q, kv[:, :HEAD], ((1,), (1,))) * (HEAD**-0.5 * LOG2E)
            parts = []
            for b in range(WINDOW // BLOCK):
                bias = jnp.where(pattern_ref[h, c, b] > 0, 0.0, -jnp.inf)
                parts.append(scores[:, b * BLOCK : (b + 1) * BLOCK] + bias)
            scores = jnp.concatenate(parts, axis=1)
            top = jnp.max(scores, axis=1, keepdims=True)
            weights = jnp.exp2(scores - top)
            total = jnp.sum(weights, axis=1, keepdims=True)
            mixed = dot(weights.astype(jnp.bfloat16), kv[:, HEAD:])
            context[pl.ds(start, CLUSTER)] = (mixed / total).astype(jnp.bfloat16)
            return carry

        lax.fori_loop(0, rows // CLUSTER, cluster, 0)
        back = dot(table(heads + h), context[...])
        leaving[h] = back.reshape(peers, share, HEAD).astype(jnp.bfloat16)
        to_all(leaving, returned, send_c, recv_c, h)

    def collect(h):
        all_of(leaving, returned, send_c, recv_c, h).wait_recv()
        came = returned[h].astype(jnp.float32).reshape(rows, HEAD).astype(jnp.bfloat16)
        gathered[plane, h] = dot(table_t(h), came).astype(jnp.bfloat16)
        ring(h, 0, 0).start()
        ring(h, 1, 0).start()

    def forward(h, hop):
        for way in (0, 1):
            if hop <= hops(h, way):
                ring(h, way, hop - 1).wait_recv()
                if hop < hops(h, way):
                    ring(h, way, hop).start()

    send_qkv(0)
    pl.semaphore_wait(barrier, peers + 1)
    start_qkv(0)
    send_qkv(1)
    start_qkv(1)
    land(0)
    send_qkv(2)
    start_qkv(2)
    attend(0)
    land(1)
    send_qkv(3)
    start_qkv(3)
    attend(1)
    collect(0)
    land(2)
    forward(0, 1)
    attend(2)
    forward(0, 2)
    collect(1)
    forward(0, 3)
    forward(1, 1)
    land(3)
    forward(0, 4)
    forward(1, 2)
    attend(3)
    collect(2)
    forward(1, 3)
    forward(2, 1)
    collect(3)
    forward(1, 4)
    forward(2, 2)
    forward(3, 1)
    forward(2, 3)
    forward(3, 2)
    forward(2, 4)
    forward(3, 3)
    forward(3, 4)

    for h in range(heads):
        all_of(packed, arrived, send_q, recv_q, h).wait_send()
        all_of(leaving, returned, send_c, recv_c, h).wait_send()
        for side in (0, 1):
            halo(h, side).wait_send()
        for way in (0, 1):
            for hop in range(hops(h, way)):
                ring(h, way, hop).wait_send()


def project_kernel(heads, a_ref, w_ref, o_ref, total):
    step = pl.program_id(0)
    here = jnp.concatenate([a_ref[0, h] for h in range(heads)], axis=1)
    part = dot(here, w_ref[...], ((1,), (1,)))

    @pl.when(step == 0)
    def _():
        total[...] = part

    @pl.when(step > 0)
    def _():
        total[...] += part

    @pl.when(step == pl.num_programs(0) - 1)
    def _():
        o_ref[...] = total[...].astype(o_ref.dtype)


def shards(queries, keys, values, route, members, pattern, w_out):
    rows = queries.shape[0]
    heads = route.shape[0]
    peers, planes = lax.axis_size("seq"), lax.axis_size("tp")
    share = rows // peers
    bf16 = jnp.bfloat16

    inner = peers // planes
    swap = []
    for y in range(planes):
        for i in range(inner):
            for z in range(planes):
                swap.append(((y * inner + i) * planes + z, (z * inner + i) * planes + y))
    turned = lax.ppermute(w_out.T, ("seq", "tp"), swap)
    weights = lax.all_gather(turned, "seq", axis=0, tiled=True)

    whole = pl.BlockSpec(memory_space=pltpu.VMEM)
    gathered = pl.pallas_call(
        functools.partial(attention_kernel, peers, planes, heads),
        out_shape=jax.ShapeDtypeStruct((planes, heads, rows, HEAD), bf16),
        in_specs=[whole] * 5 + [pl.BlockSpec(memory_space=pltpu.SMEM)],
        out_specs=whole,
        scratch_shapes=[
            pltpu.VMEM((2 * heads, rows), jnp.int32),
            pltpu.VMEM((rows, 2 * heads), jnp.int32),
            pltpu.VMEM((heads, peers, share, 3 * HEAD), bf16),
            pltpu.VMEM((heads, peers, share, 3 * HEAD), bf16),
            pltpu.VMEM((heads, rows, HEAD), bf16),
            pltpu.VMEM((heads, 3 * rows, 2 * HEAD), bf16),
            pltpu.VMEM((rows, HEAD), bf16),
            pltpu.VMEM((heads, peers, share, HEAD), bf16),
            pltpu.VMEM((heads, peers, share, HEAD), bf16),
            pltpu.SemaphoreType.DMA((heads,)),
            pltpu.SemaphoreType.DMA((heads,)),
            pltpu.SemaphoreType.DMA((heads, 2)),
            pltpu.SemaphoreType.DMA((heads, 2)),
            pltpu.SemaphoreType.DMA((heads,)),
            pltpu.SemaphoreType.DMA((heads,)),
            pltpu.SemaphoreType.DMA((heads, 2, planes // 2)),
            pltpu.SemaphoreType.DMA((heads, 2, planes // 2)),
        ],
        compiler_params=pltpu.CompilerParams(
            collective_id=0, has_side_effects=True, vmem_limit_bytes=48 * 2**20
        ),
        cost_estimate=pl.CostEstimate(
            flops=4 * 10**9, bytes_accessed=6 * 2**20, transcendentals=3 * 10**6
        ),
    )(queries, keys, values, route, members, pattern)

    return pl.pallas_call(
        functools.partial(project_kernel, heads),
        grid=(planes,),
        out_shape=jax.ShapeDtypeStruct((rows, rows), bf16),
        in_specs=[
            pl.BlockSpec((1, heads, rows, HEAD), lambda g: (g, 0, 0, 0)),
            pl.BlockSpec((rows, heads * HEAD), lambda g: (g, 0)),
        ],
        out_specs=pl.BlockSpec((rows, rows), lambda g: (0, 0)),
        scratch_shapes=[pltpu.VMEM((rows, rows), jnp.float32)],
        compiler_params=pltpu.CompilerParams(vmem_limit_bytes=16 * 2**20),
    )(gathered, weights)


def solution(mesh):
    placed = (
        P("seq", "tp"),
        P("seq", "tp"),
        P("seq", "tp"),
        P("tp", "seq"),
        P("tp", "seq"),
        P("tp", "seq", None),
        P("tp", "seq"),
    )
    return jax.shard_map(
        shards, mesh=mesh, in_specs=placed, out_specs=P("seq", "tp"), check_vma=False
    )
```

```python
import functools

import jax
import jax.numpy as jnp
from jax import lax
from jax.experimental import pallas as pl
from jax.experimental.pallas import tpu as pltpu
from jax.sharding import PartitionSpec as P

MESH = pl.DeviceIdType.MESH
HEAD = 128
CLUSTER = 256
BLOCK = 128
WINDOW = 5 * CLUSTER
LOG2E = 1.4426950408889634


def dot(a, b, contract=((1,), (0,))):
    return lax.dot_general(a, b, (contract, ((), ())), preferred_element_type=jnp.float32)


def layer_kernel(
    peers, planes, heads,
    q_hbm, k_hbm, v_hbm, route_hbm, members_hbm, pattern_hbm, w_hbm,
    mixed,
    q_ref, k_ref, v_ref, route_ref, members_ref, pattern_ref,
    index_row, index_col, packed, arrived, query, window, context, leaving, returned,
    gathered, weights, total,
    load, send_q, recv_q, send_h, recv_h, send_c, recv_c, send_z, recv_z, send_w, recv_w,
):
    rows = q_ref.shape[0]
    share = rows // peers
    inner = peers // planes
    me = lax.axis_index("seq")
    plane = lax.axis_index("tp")
    after, before = me + 1, me - 1
    above, below = lax.rem(plane + 1, planes), lax.rem(plane + planes - 1, planes)
    line, place = lax.div(me, inner), lax.rem(me, inner)
    column, core = lax.div(place, 2), lax.rem(place, 2)
    columns = inner // 2
    sibling = me + 1 - 2 * core
    has_before, has_after = me > 0, me < peers - 1
    turned = line != plane

    loads = [
        pltpu.make_async_copy(source, target, load.at[i])
        for i, (source, target) in enumerate(
            (
                (route_hbm, route_ref),
                (members_hbm, members_ref),
                (q_hbm, q_ref),
                (k_hbm, k_ref),
                (v_hbm, v_ref),
                (pattern_hbm, pattern_ref),
            )
        )
    ]
    for copy in loads:
        copy.start()

    barrier = pltpu.get_barrier_semaphore()

    def greet(i, carry):
        pl.semaphore_signal(
            barrier, inc=1, device_id={"seq": lax.rem(me + i, peers)}, device_id_type=MESH
        )
        return carry

    lax.fori_loop(1, peers, greet, 0)
    for other in (above, below):
        pl.semaphore_signal(barrier, inc=1, device_id={"tp": other}, device_id_type=MESH)

    mirror = {"seq": plane * inner + place, "tp": line}

    @pl.when(turned)
    def _():
        pl.semaphore_signal(barrier, inc=1, device_id=mirror, device_id_type=MESH)

    def meet():
        @pl.when(turned)
        def _():
            pl.semaphore_wait(barrier, peers + 2)

        @pl.when(jnp.logical_not(turned))
        def _():
            pl.semaphore_wait(barrier, peers + 1)

    def rank(i, order, order_col):
        smaller = order_col[:, i : i + 1] < order[i : i + 1, :]
        return jnp.sum(smaller.astype(jnp.float32), axis=0, keepdims=True)

    def table(i):
        at = lax.broadcasted_iota(jnp.int32, (rows, rows), 0)
        return (at == index_row[i : i + 1, :]).astype(jnp.bfloat16)

    def table_t(i):
        at = lax.broadcasted_iota(jnp.int32, (rows, rows), 1)
        return (at == index_col[:, i : i + 1]).astype(jnp.bfloat16)

    def to_all(source, landing, send_sem, recv_sem, h):
        def send(i, carry):
            peer = lax.rem(me + i, peers)
            pltpu.make_async_remote_copy(
                src_ref=source.at[h, peer], dst_ref=landing.at[h, me],
                send_sem=send_sem.at[h], recv_sem=recv_sem.at[h],
                device_id={"seq": peer}, device_id_type=MESH,
            ).start()
            return carry

        lax.fori_loop(1, peers, send, 0)
        landing[h, me] = source[h, me]

    def all_of(source, landing, send_sem, recv_sem, h):
        others = pl.ds(0, peers - 1)
        return pltpu.make_async_remote_copy(
            src_ref=source.at[h, others], dst_ref=landing.at[h, others],
            send_sem=send_sem.at[h], recv_sem=recv_sem.at[h],
            device_id={"seq": sibling}, device_id_type=MESH,
        )

    def halo(h, side):
        own = window.at[h, pl.ds(rows, rows)]
        landing = window.at[h, pl.ds(0 if side == 0 else 2 * rows, rows)]
        return pltpu.make_async_remote_copy(
            src_ref=own, dst_ref=landing,
            send_sem=send_h.at[h, side], recv_sem=recv_h.at[h, side],
            device_id={"seq": after if side == 0 else before}, device_id_type=MESH,
        )

    def hops(h, way):
        return planes // 2 - (h + way) % 2

    def ring(h, way, hop):
        held = lax.rem(plane + planes - hop if way == 0 else plane + hop, planes)
        block = gathered.at[held, h]
        return pltpu.make_async_remote_copy(
            src_ref=block, dst_ref=block,
            send_sem=send_z.at[h, way, hop], recv_sem=recv_z.at[h, way, hop],
            device_id={"tp": above if way == 0 else below}, device_id_type=MESH,
        )

    def w_copy(i, block, to):
        return pltpu.make_async_remote_copy(
            src_ref=block, dst_ref=block, send_sem=send_w.at[i], recv_sem=recv_w.at[i],
            device_id={"seq": to}, device_id_type=MESH,
        )

    def w_turn():
        return pltpu.make_async_remote_copy(
            src_ref=w_hbm, dst_ref=weights.at[plane, place],
            send_sem=send_w.at[0], recv_sem=recv_w.at[0],
            device_id=mirror, device_id_type=MESH,
        )

    def w_line(way, hop):
        held = lax.rem(line + planes - hop if way == 0 else line + hop, planes)
        to = lax.rem(line + (1 if way == 0 else planes - 1), planes)
        return w_copy(1 + way * 4 + hop, weights.at[held, place], to * inner + place)

    def beside(step):
        return lax.rem(column + columns + step, columns)

    def w_near(way):
        to = beside(1 if way == 0 else -1)
        return w_copy(9 + way, weights.at[:, place], line * inner + to * 2 + core)

    def w_far(way):
        to, held = (beside(1), beside(-1)) if way == 0 else (beside(-1), beside(1))
        half = pl.ds(way * (planes // 2), planes // 2)
        return w_copy(11 + way, weights.at[half, held * 2 + core], line * inner + to * 2 + core)

    def w_pair(step):
        return w_copy(13 + step, weights.at[:, beside(step) * 2 + core], sibling)

    def w_begin():
        @pl.when(turned)
        def _():
            w_turn().start()

        @pl.when(jnp.logical_not(turned))
        def _():
            pltpu.make_async_copy(w_hbm, weights.at[plane, place], recv_w.at[0]).start()

    def w_step(hop):
        if hop == 0:
            w_turn().wait_recv()
        for way in (0, 1):
            if 0 < hop <= 4 - way:
                w_line(way, hop - 1).wait_recv()
            if hop < 4 - way:
                w_line(way, hop).start()
        if hop == 4:
            w_near(0).start()
            w_near(1).start()
            w_pair(0).start()
        if hop == 5:
            w_near(0).wait_recv()
            w_near(1).wait_recv()
            w_far(0).start()
            w_far(1).start()
            w_pair(1).start()
            w_pair(3).start()
        if hop == 6:
            w_far(0).wait_recv()
            w_far(1).wait_recv()
            w_pair(2).start()
        if hop == 7:
            for step in range(columns):
                w_pair(step).wait_recv()

    def pack(h):
        at = slice(h * HEAD, (h + 1) * HEAD)
        stacked = jnp.concatenate([q_ref[:, at], k_ref[:, at], v_ref[:, at]], axis=1)
        packed[h] = dot(table(h), stacked).reshape(peers, share, 3 * HEAD).astype(jnp.bfloat16)

    def send(h):
        to_all(packed, arrived, send_q, recv_q, h)

    def land(h):
        all_of(packed, arrived, send_q, recv_q, h).wait_recv()
        came = arrived[h].astype(jnp.float32).reshape(rows, 3 * HEAD).astype(jnp.bfloat16)
        placed = dot(table_t(heads + h), came).astype(jnp.bfloat16)
        window[h, pl.ds(rows, rows)] = placed[:, HEAD:]

        @pl.when(has_after)
        def _():
            halo(h, 0).start()

        @pl.when(has_before)
        def _():
            halo(h, 1).start()

        query[h] = placed[:, :HEAD]

    def attend(h):
        @pl.when(has_before)
        def _():
            halo(h, 0).wait_recv()

        @pl.when(has_after)
        def _():
            halo(h, 1).wait_recv()

        def cluster(c, carry):
            start = pl.multiple_of(c * CLUSTER, CLUSTER)
            q = query[h, pl.ds(start, CLUSTER)]
            kv = window.at[h, pl.ds(start, WINDOW)]
            scores = dot(q, kv[:, :HEAD], ((1,), (1,))) * (HEAD**-0.5 * LOG2E)
            parts = []
            for b in range(WINDOW // BLOCK):
                bias = jnp.where(pattern_ref[h, c, b] > 0, 0.0, -jnp.inf)
                parts.append(scores[:, b * BLOCK : (b + 1) * BLOCK] + bias)
            scores = jnp.concatenate(parts, axis=1)
            top = jnp.max(scores, axis=1, keepdims=True)
            chances = jnp.exp2(scores - top)
            mass = jnp.sum(chances, axis=1, keepdims=True)
            summed = dot(chances.astype(jnp.bfloat16), kv[:, HEAD:])
            context[pl.ds(start, CLUSTER)] = (summed / mass).astype(jnp.bfloat16)
            return carry

        lax.fori_loop(0, rows // CLUSTER, cluster, 0)
        back = dot(table(heads + h), context[...])
        leaving[h] = back.reshape(peers, share, HEAD).astype(jnp.bfloat16)
        to_all(leaving, returned, send_c, recv_c, h)

    def collect(h):
        all_of(leaving, returned, send_c, recv_c, h).wait_recv()
        came = returned[h].astype(jnp.float32).reshape(rows, HEAD).astype(jnp.bfloat16)
        gathered[plane, h] = dot(table_t(h), came).astype(jnp.bfloat16)
        ring(h, 0, 0).start()
        ring(h, 1, 0).start()

    def forward(h, hop):
        for way in (0, 1):
            if hop <= hops(h, way):
                ring(h, way, hop - 1).wait_recv()
                if hop < hops(h, way):
                    ring(h, way, hop).start()

    def project(group, first):
        held = lax.rem(plane + group, planes)
        here = jnp.concatenate([gathered[held, first], gathered[held, first + 1]], axis=1)
        block = weights[held, :, :, first * HEAD : (first + 2) * HEAD].reshape(rows, 2 * HEAD)
        return dot(here, block, ((1,), (1,)))

    loads[0].wait()
    loads[1].wait()
    slot = lax.broadcasted_iota(jnp.int32, members_ref.shape, 1)
    order = jnp.concatenate(
        [route_ref[...], lax.div(members_ref[...], rows) * rows + slot], axis=0
    ).astype(jnp.float32)
    order_col = order.T
    ranks = [rank(0, order, order_col)]
    index_row[0:1, :] = ranks[0].astype(jnp.int32)
    for copy in loads[2:]:
        copy.wait()
    pack(0)
    meet()
    send(0)
    for i in range(1, 2 * heads):
        ranks.append(rank(i, order, order_col))
        index_row[i : i + 1, :] = ranks[i].astype(jnp.int32)
        if i == 1:
            pack(1)
            send(1)
    index_col[...] = jnp.concatenate(ranks, axis=0).T.astype(jnp.int32)

    @pl.when(jnp.logical_not(has_before))
    def _():
        for h in range(heads):
            window[h, pl.ds(0, rows)] = jnp.zeros((rows, 2 * HEAD), jnp.bfloat16)

    @pl.when(jnp.logical_not(has_after))
    def _():
        for h in range(heads):
            window[h, pl.ds(2 * rows, rows)] = jnp.zeros((rows, 2 * HEAD), jnp.bfloat16)

    land(0)
    pack(2)
    send(2)
    w_begin()
    attend(0)
    land(1)
    pack(3)
    send(3)
    w_step(0)
    attend(1)
    collect(0)
    w_step(1)
    land(2)
    forward(0, 1)
    w_step(2)
    attend(2)
    collect(1)
    forward(0, 2)
    w_step(3)
    land(3)
    forward(0, 3)
    forward(1, 1)
    w_step(4)
    attend(3)
    collect(2)
    forward(1, 2)
    forward(0, 4)
    w_step(5)
    forward(2, 1)
    forward(1, 3)
    collect(3)
    forward(2, 2)
    forward(3, 1)
    w_step(6)
    forward(1, 4)
    forward(2, 3)
    forward(3, 2)
    w_step(7)
    total[...] = project(0, 0)
    def add(group, carry):
        total[...] += project(group, 0)
        return carry

    forward(2, 4)
    lax.fori_loop(1, planes, add, 0)
    total[...] += project(0, 2)
    for hop in (1, 2):
        total[...] += project(planes - hop, 2)
        total[...] += project(hop, 2)
    forward(3, 3)
    total[...] += project(planes - 3, 2)
    total[...] += project(3, 2)
    forward(3, 4)
    total[...] += project(4, 2)

    for h in range(heads):
        all_of(packed, arrived, send_q, recv_q, h).wait_send()
        all_of(leaving, returned, send_c, recv_c, h).wait_send()

        @pl.when(has_after)
        def _():
            halo(h, 0).wait_send()

        @pl.when(has_before)
        def _():
            halo(h, 1).wait_send()

        for way in (0, 1):
            for hop in range(hops(h, way)):
                ring(h, way, hop).wait_send()

    @pl.when(turned)
    def _():
        w_turn().wait_send()

    for way in (0, 1):
        for hop in range(4 - way):
            w_line(way, hop).wait_send()
        w_near(way).wait_send()
        w_far(way).wait_send()
    for step in range(columns):
        w_pair(step).wait_send()
    mixed[...] = total[...].astype(mixed.dtype)


def shards(queries, keys, values, route, members, pattern, w_out):
    rows = queries.shape[0]
    heads = route.shape[0]
    peers, planes = lax.axis_size("seq"), lax.axis_size("tp")
    share, inner = rows // peers, peers // planes
    bf16 = jnp.bfloat16
    vmem, dma = pltpu.VMEM, pltpu.SemaphoreType.DMA
    return pl.pallas_call(
        functools.partial(layer_kernel, peers, planes, heads),
        out_shape=jax.ShapeDtypeStruct((rows, rows), bf16),
        in_specs=[pl.BlockSpec(memory_space=pltpu.HBM)] * 7,
        out_specs=pl.BlockSpec(memory_space=pltpu.VMEM),
        scratch_shapes=[
            vmem(queries.shape, bf16),
            vmem(keys.shape, bf16),
            vmem(values.shape, bf16),
            vmem(route.shape, jnp.int32),
            vmem(members.shape, jnp.int32),
            pltpu.SMEM(pattern.shape, jnp.int32),
            vmem((2 * heads, rows), jnp.int32),
            vmem((rows, 2 * heads), jnp.int32),
            vmem((heads, peers, share, 3 * HEAD), bf16),
            vmem((heads, peers, share, 3 * HEAD), bf16),
            vmem((heads, rows, HEAD), bf16),
            vmem((heads, 3 * rows, 2 * HEAD), bf16),
            vmem((rows, HEAD), bf16),
            vmem((heads, peers, share, HEAD), bf16),
            vmem((heads, peers, share, HEAD), bf16),
            vmem((planes, heads, rows, HEAD), bf16),
            vmem((planes, inner, rows // inner, heads * HEAD), bf16),
            vmem((rows, rows), jnp.float32),
            dma((6,)),
            dma((heads,)),
            dma((heads,)),
            dma((heads, 2)),
            dma((heads, 2)),
            dma((heads,)),
            dma((heads,)),
            dma((heads, 2, planes // 2)),
            dma((heads, 2, planes // 2)),
            dma((17,)),
            dma((17,)),
        ],
        compiler_params=pltpu.CompilerParams(
            collective_id=0, has_side_effects=True, vmem_limit_bytes=56 * 2**20
        ),
        cost_estimate=pl.CostEstimate(
            flops=7 * 10**9, bytes_accessed=3 * 2**20, transcendentals=3 * 10**6
        ),
    )(queries, keys, values, route, members, pattern, w_out.T)


def solution(mesh):
    placed = (
        P("seq", "tp"),
        P("seq", "tp"),
        P("seq", "tp"),
        P("tp", "seq"),
        P("tp", "seq"),
        P("tp", "seq", None),
        P("tp", "seq"),
    )
    return jax.shard_map(
        shards, mesh=mesh, in_specs=placed, out_specs=P("seq", "tp"), check_vma=False
    )
```

```python
import functools

import jax
import jax.numpy as jnp
from jax import lax
from jax.experimental import pallas as pl
from jax.experimental.pallas import tpu as pltpu
from jax.sharding import PartitionSpec as P

MESH = pl.DeviceIdType.MESH
HEAD = 128
CLUSTER = 256
BLOCK = 128
WINDOW = 5 * CLUSTER
LOG2E = 1.4426950408889634


def dot(a, b, contract=((1,), (0,))):
    return lax.dot_general(a, b, (contract, ((), ())), preferred_element_type=jnp.float32)


def layer_kernel(
    peers, planes, heads,
    q_hbm, k_hbm, v_hbm, route_hbm, members_hbm, pattern_hbm, w_hbm,
    mixed,
    q_ref, k_ref, v_ref, route_ref, members_ref, pattern_ref,
    index_row, index_col, packed, arrived, query, window, context, leaving, returned,
    gathered, weights, total,
    load, send_q, recv_q, send_h, recv_h, send_c, recv_c, send_z, recv_z, send_w, recv_w,
):
    rows = q_ref.shape[0]
    share = rows // peers
    inner = peers // planes
    me = lax.axis_index("seq")
    plane = lax.axis_index("tp")
    after, before = me + 1, me - 1
    above, below = lax.rem(plane + 1, planes), lax.rem(plane + planes - 1, planes)
    line, place = lax.div(me, inner), lax.rem(me, inner)
    column, core = lax.div(place, 2), lax.rem(place, 2)
    columns = inner // 2
    sibling = me + 1 - 2 * core
    has_before, has_after = me > 0, me < peers - 1
    turned = line != plane

    loads = [
        pltpu.make_async_copy(source, target, load.at[i])
        for i, (source, target) in enumerate(
            (
                (route_hbm, route_ref),
                (members_hbm, members_ref),
                (q_hbm, q_ref),
                (k_hbm, k_ref),
                (v_hbm, v_ref),
                (pattern_hbm, pattern_ref),
            )
        )
    ]
    for copy in loads:
        copy.start()

    barrier = pltpu.get_barrier_semaphore()

    def greet(i, carry):
        pl.semaphore_signal(
            barrier, inc=1, device_id={"seq": lax.rem(me + i, peers)}, device_id_type=MESH
        )
        return carry

    lax.fori_loop(1, peers, greet, 0)
    for other in (above, below):
        pl.semaphore_signal(barrier, inc=1, device_id={"tp": other}, device_id_type=MESH)

    mirror = {"seq": plane * inner + place, "tp": line}

    @pl.when(turned)
    def _():
        pl.semaphore_signal(barrier, inc=1, device_id=mirror, device_id_type=MESH)

    def meet():
        @pl.when(turned)
        def _():
            pl.semaphore_wait(barrier, peers + 2)

        @pl.when(jnp.logical_not(turned))
        def _():
            pl.semaphore_wait(barrier, peers + 1)

    def rank(i, order, order_col):
        smaller = order_col[:, i : i + 1] < order[i : i + 1, :]
        return jnp.sum(smaller.astype(jnp.float32), axis=0, keepdims=True)

    def table(i):
        at = lax.broadcasted_iota(jnp.int32, (rows, rows), 0)
        return (at == index_row[i : i + 1, :]).astype(jnp.bfloat16)

    def table_t(i):
        at = lax.broadcasted_iota(jnp.int32, (rows, rows), 1)
        return (at == index_col[:, i : i + 1]).astype(jnp.bfloat16)

    def to_all(source, landing, send_sem, recv_sem, h):
        def send(i, carry):
            peer = lax.rem(me + i, peers)
            pltpu.make_async_remote_copy(
                src_ref=source.at[h, peer], dst_ref=landing.at[h, me],
                send_sem=send_sem.at[h], recv_sem=recv_sem.at[h],
                device_id={"seq": peer}, device_id_type=MESH,
            ).start()
            return carry

        lax.fori_loop(1, peers, send, 0)
        landing[h, me] = source[h, me]

    def all_of(source, landing, send_sem, recv_sem, h):
        others = pl.ds(0, peers - 1)
        return pltpu.make_async_remote_copy(
            src_ref=source.at[h, others], dst_ref=landing.at[h, others],
            send_sem=send_sem.at[h], recv_sem=recv_sem.at[h],
            device_id={"seq": sibling}, device_id_type=MESH,
        )

    def halo(h, side):
        own = window.at[h, pl.ds(rows, rows)]
        landing = window.at[h, pl.ds(0 if side == 0 else 2 * rows, rows)]
        return pltpu.make_async_remote_copy(
            src_ref=own, dst_ref=landing,
            send_sem=send_h.at[h, side], recv_sem=recv_h.at[h, side],
            device_id={"seq": after if side == 0 else before}, device_id_type=MESH,
        )

    def hops(h, way):
        return planes // 2 - (h + way) % 2

    def ring(h, way, hop):
        held = lax.rem(plane + planes - hop if way == 0 else plane + hop, planes)
        block = gathered.at[held, h]
        return pltpu.make_async_remote_copy(
            src_ref=block, dst_ref=block,
            send_sem=send_z.at[h, way, hop], recv_sem=recv_z.at[h, way, hop],
            device_id={"tp": above if way == 0 else below}, device_id_type=MESH,
        )

    def w_copy(i, block, to):
        return pltpu.make_async_remote_copy(
            src_ref=block, dst_ref=block, send_sem=send_w.at[i], recv_sem=recv_w.at[i],
            device_id={"seq": to}, device_id_type=MESH,
        )

    def w_turn():
        return pltpu.make_async_remote_copy(
            src_ref=w_hbm, dst_ref=weights.at[plane, place],
            send_sem=send_w.at[0], recv_sem=recv_w.at[0],
            device_id=mirror, device_id_type=MESH,
        )

    def w_line(way, hop):
        held = lax.rem(line + planes - hop if way == 0 else line + hop, planes)
        to = lax.rem(line + (1 if way == 0 else planes - 1), planes)
        return w_copy(1 + way * 4 + hop, weights.at[held, place], to * inner + place)

    def beside(step):
        return lax.rem(column + columns + step, columns)

    def w_near(way):
        to = beside(1 if way == 0 else -1)
        return w_copy(9 + way, weights.at[:, place], line * inner + to * 2 + core)

    def w_far(way):
        to, held = (beside(1), beside(-1)) if way == 0 else (beside(-1), beside(1))
        half = pl.ds(way * (planes // 2), planes // 2)
        return w_copy(11 + way, weights.at[half, held * 2 + core], line * inner + to * 2 + core)

    def w_pair(step):
        return w_copy(13 + step, weights.at[:, beside(step) * 2 + core], sibling)

    def w_begin():
        @pl.when(turned)
        def _():
            w_turn().start()

        @pl.when(jnp.logical_not(turned))
        def _():
            pltpu.make_async_copy(w_hbm, weights.at[plane, place], recv_w.at[0]).start()

    def w_step(hop):
        if hop == 0:
            w_turn().wait_recv()
        for way in (0, 1):
            if 0 < hop <= 4 - way:
                w_line(way, hop - 1).wait_recv()
            if hop < 4 - way:
                w_line(way, hop).start()
        if hop == 4:
            w_near(0).start()
            w_near(1).start()
            w_pair(0).start()
        if hop == 5:
            w_near(0).wait_recv()
            w_near(1).wait_recv()
            w_far(0).start()
            w_far(1).start()
            w_pair(1).start()
            w_pair(3).start()
        if hop == 6:
            w_far(0).wait_recv()
            w_far(1).wait_recv()
            w_pair(2).start()
        if hop == 7:
            for step in range(columns):
                w_pair(step).wait_recv()

    def pack(h):
        at = slice(h * HEAD, (h + 1) * HEAD)
        stacked = jnp.concatenate([q_ref[:, at], k_ref[:, at], v_ref[:, at]], axis=1)
        packed[h] = dot(table(h), stacked).reshape(peers, share, 3 * HEAD).astype(jnp.bfloat16)

    def send(h):
        to_all(packed, arrived, send_q, recv_q, h)

    def land(h):
        all_of(packed, arrived, send_q, recv_q, h).wait_recv()
        came = arrived[h].astype(jnp.float32).reshape(rows, 3 * HEAD).astype(jnp.bfloat16)
        placed = dot(table_t(heads + h), came).astype(jnp.bfloat16)
        window[h, pl.ds(rows, rows)] = placed[:, HEAD:]

        @pl.when(has_after)
        def _():
            halo(h, 0).start()

        @pl.when(has_before)
        def _():
            halo(h, 1).start()

        query[h] = placed[:, :HEAD]

    def attend(h):
        @pl.when(has_before)
        def _():
            halo(h, 0).wait_recv()

        @pl.when(has_after)
        def _():
            halo(h, 1).wait_recv()

        def cluster(c, carry):
            start = pl.multiple_of(c * CLUSTER, CLUSTER)
            q = query[h, pl.ds(start, CLUSTER)]
            kv = window.at[h, pl.ds(start, WINDOW)]
            scores = dot(q, kv[:, :HEAD], ((1,), (1,))) * (HEAD**-0.5 * LOG2E)
            parts = []
            for b in range(WINDOW // BLOCK):
                bias = jnp.where(pattern_ref[h, c, b] > 0, 0.0, -jnp.inf)
                parts.append(scores[:, b * BLOCK : (b + 1) * BLOCK] + bias)
            scores = jnp.concatenate(parts, axis=1)
            top = jnp.max(scores, axis=1, keepdims=True)
            chances = jnp.exp2(scores - top)
            mass = jnp.sum(chances, axis=1, keepdims=True)
            summed = dot(chances.astype(jnp.bfloat16), kv[:, HEAD:])
            context[pl.ds(start, CLUSTER)] = (summed / mass).astype(jnp.bfloat16)
            return carry

        lax.fori_loop(0, rows // CLUSTER, cluster, 0)
        back = dot(table(heads + h), context[...])
        leaving[h] = back.reshape(peers, share, HEAD).astype(jnp.bfloat16)
        to_all(leaving, returned, send_c, recv_c, h)

    def collect(h):
        all_of(leaving, returned, send_c, recv_c, h).wait_recv()
        came = returned[h].astype(jnp.float32).reshape(rows, HEAD).astype(jnp.bfloat16)
        gathered[plane, h] = dot(table_t(h), came).astype(jnp.bfloat16)
        ring(h, 0, 0).start()
        ring(h, 1, 0).start()

    def forward(h, hop):
        for way in (0, 1):
            if hop <= hops(h, way):
                ring(h, way, hop - 1).wait_recv()
                if hop < hops(h, way):
                    ring(h, way, hop).start()

    def project(group, first):
        held = lax.rem(plane + group, planes)
        here = jnp.concatenate([gathered[held, first], gathered[held, first + 1]], axis=1)
        block = weights[held, :, :, first * HEAD : (first + 2) * HEAD].reshape(rows, 2 * HEAD)
        return dot(here, block, ((1,), (1,)))

    loads[0].wait()
    loads[1].wait()
    slot = lax.broadcasted_iota(jnp.int32, members_ref.shape, 1)
    order = jnp.concatenate(
        [route_ref[...], lax.div(members_ref[...], rows) * rows + slot], axis=0
    ).astype(jnp.float32)
    order_col = order.T
    ranks = [rank(0, order, order_col)]
    index_row[0:1, :] = ranks[0].astype(jnp.int32)
    for copy in loads[2:]:
        copy.wait()
    pack(0)
    meet()
    send(0)
    for i in range(1, 2 * heads):
        ranks.append(rank(i, order, order_col))
        index_row[i : i + 1, :] = ranks[i].astype(jnp.int32)
        if i == 1:
            pack(1)
            send(1)
    index_col[...] = jnp.concatenate(ranks, axis=0).T.astype(jnp.int32)

    @pl.when(jnp.logical_not(has_before))
    def _():
        for h in range(heads):
            window[h, pl.ds(0, rows)] = jnp.zeros((rows, 2 * HEAD), jnp.bfloat16)

    @pl.when(jnp.logical_not(has_after))
    def _():
        for h in range(heads):
            window[h, pl.ds(2 * rows, rows)] = jnp.zeros((rows, 2 * HEAD), jnp.bfloat16)

    land(0)
    pack(2)
    send(2)
    w_begin()
    attend(0)
    land(1)
    pack(3)
    send(3)
    w_step(0)
    attend(1)
    collect(0)
    w_step(1)
    land(2)
    forward(0, 1)
    w_step(2)
    attend(2)
    collect(1)
    forward(0, 2)
    w_step(3)
    land(3)
    forward(0, 3)
    forward(1, 1)
    w_step(4)
    attend(3)
    collect(2)
    forward(1, 2)
    forward(0, 4)
    w_step(5)
    forward(2, 1)
    forward(1, 3)
    collect(3)
    forward(2, 2)
    forward(3, 1)
    w_step(6)
    forward(1, 4)
    forward(2, 3)
    forward(3, 2)
    w_step(7)
    forward(2, 4)

    def add(group, carry):
        total[...] += project(group, 0)
        return carry

    total[...] = project(0, 0)
    lax.fori_loop(1, 4, add, 0)
    forward(3, 3)
    lax.fori_loop(4, planes, add, 0)
    total[...] += project(0, 2)
    for hop in (1, 2, 3):
        total[...] += project(planes - hop, 2)
        total[...] += project(hop, 2)
    forward(3, 4)
    total[...] += project(4, 2)

    for h in range(heads):
        all_of(packed, arrived, send_q, recv_q, h).wait_send()
        all_of(leaving, returned, send_c, recv_c, h).wait_send()

        @pl.when(has_after)
        def _():
            halo(h, 0).wait_send()

        @pl.when(has_before)
        def _():
            halo(h, 1).wait_send()

        for way in (0, 1):
            for hop in range(hops(h, way)):
                ring(h, way, hop).wait_send()

    @pl.when(turned)
    def _():
        w_turn().wait_send()

    for way in (0, 1):
        for hop in range(4 - way):
            w_line(way, hop).wait_send()
        w_near(way).wait_send()
        w_far(way).wait_send()
    for step in range(columns):
        w_pair(step).wait_send()
    mixed[...] = total[...].astype(mixed.dtype)


def shards(queries, keys, values, route, members, pattern, w_out):
    rows = queries.shape[0]
    heads = route.shape[0]
    peers, planes = lax.axis_size("seq"), lax.axis_size("tp")
    share, inner = rows // peers, peers // planes
    bf16 = jnp.bfloat16
    vmem, dma = pltpu.VMEM, pltpu.SemaphoreType.DMA
    return pl.pallas_call(
        functools.partial(layer_kernel, peers, planes, heads),
        out_shape=jax.ShapeDtypeStruct((rows, rows), bf16),
        in_specs=[pl.BlockSpec(memory_space=pltpu.HBM)] * 7,
        out_specs=pl.BlockSpec(memory_space=pltpu.VMEM),
        scratch_shapes=[
            vmem(queries.shape, bf16),
            vmem(keys.shape, bf16),
            vmem(values.shape, bf16),
            vmem(route.shape, jnp.int32),
            vmem(members.shape, jnp.int32),
            pltpu.SMEM(pattern.shape, jnp.int32),
            vmem((2 * heads, rows), jnp.int32),
            vmem((rows, 2 * heads), jnp.int32),
            vmem((heads, peers, share, 3 * HEAD), bf16),
            vmem((heads, peers, share, 3 * HEAD), bf16),
            vmem((heads, rows, HEAD), bf16),
            vmem((heads, 3 * rows, 2 * HEAD), bf16),
            vmem((rows, HEAD), bf16),
            vmem((heads, peers, share, HEAD), bf16),
            vmem((heads, peers, share, HEAD), bf16),
            vmem((planes, heads, rows, HEAD), bf16),
            vmem((planes, inner, rows // inner, heads * HEAD), bf16),
            vmem((rows, rows), jnp.float32),
            dma((6,)),
            dma((heads,)),
            dma((heads,)),
            dma((heads, 2)),
            dma((heads, 2)),
            dma((heads,)),
            dma((heads,)),
            dma((heads, 2, planes // 2)),
            dma((heads, 2, planes // 2)),
            dma((17,)),
            dma((17,)),
        ],
        compiler_params=pltpu.CompilerParams(
            collective_id=0, has_side_effects=True, vmem_limit_bytes=56 * 2**20
        ),
        cost_estimate=pl.CostEstimate(
            flops=7 * 10**9, bytes_accessed=3 * 2**20, transcendentals=3 * 10**6
        ),
    )(queries, keys, values, route, members, pattern, w_out.T)


def solution(mesh):
    placed = (
        P("seq", "tp"),
        P("seq", "tp"),
        P("seq", "tp"),
        P("tp", "seq"),
        P("tp", "seq"),
        P("tp", "seq", None),
        P("tp", "seq"),
    )
    return jax.shard_map(
        shards, mesh=mesh, in_specs=placed, out_specs=P("seq", "tp"), check_vma=False
    )
```
